32 devices in a mesh: tm: 4 (over z), row: 8 (over y, x, core).
Axes of the slice: x: 2, y: 2, z: 4, core: 2. Of those that a mesh axis runs over, the one named last changes fastest.
Arguments:
- solution: float32 [4, 16, 8192], P('tm', None, 'row'), may hold values from -6 to 6
- residual: float32 [4, 16, 8192], P('tm', None, 'row'), may hold values from -6 to 6
- direction: float32 [4, 16, 8192], P('tm', None, 'row'), may hold values from -6 to 6
- normal: bfloat16 [4, 8192, 8192], P('tm', 'row'), as said below
- weights: float32 [8192], P('row'), may hold values from 0.3 to 3
Outputs:
- new_solution: float32 [4, 16, 8192], P('tm', None, 'row')
- new_residual: float32 [4, 16, 8192], P('tm', None, 'row')
- new_direction: float32 [4, 16, 8192], P('tm', None, 'row')
The draws below stay inside these ranges and needn't reach their ends.
Inputs may be any that keep to these rules, and one draw needn't show every extreme that they name: `normal`: each month's block of 8192 x 8192 is symmetric and positive definite.
All inputs are finite; a program needn't handle non-finite values.
Results may differ from the reference program's by a relative error of at most 0.0026.
Values may be sent and summed in bfloat16 or wider, within the bound.
No kernel may reach another device: no remote copies, remote signals or barrier semaphores. Data moves between devices by JAX's collectives and lax.ppermute only.
A program may use at most 64 MiB of HBM per device.

```python
import math
import jax
import jax.numpy as jnp
from jax import lax

RHS = 16
COEFFS = 8192
MONTHS = 4


factor_count = 16


factor_scale = 0.07


def draw_normal(key, part):
    key = jax.random.fold_in(key, 7)

    def month(index):
        month_key = jax.random.fold_in(key, index)
        key_base = jax.random.fold_in(month_key, 0)
        key_diag = jax.random.fold_in(month_key, 1)
        key_factor = jax.random.fold_in(month_key, 3)
        key_phase = jax.random.fold_in(month_key, 4)
        rows = lax.broadcasted_iota(jnp.int32, (COEFFS, COEFFS), 0)
        cols = lax.broadcasted_iota(jnp.int32, (COEFFS, COEFFS), 1)
        spread = 0.7 / math.sqrt(COEFFS)
        base = jax.random.normal(key_base, (COEFFS, COEFFS), jnp.float32)
        upper = jnp.where(rows <= cols, base, base.T) * spread
        diag = jax.random.uniform(key_diag, (COEFFS,), jnp.float32, 2.5, 5.0)
        matrix = jnp.where(rows == cols, diag[:, None], upper)
        positions = jnp.arange(COEFFS, dtype=jnp.float32)
        frequency = jnp.arange(1, factor_count + 1, dtype=jnp.float32)
        phases = jax.random.uniform(key_phase, (factor_count,), jnp.float32, 0.0, 2.0 * math.pi)
        wave_part = jnp.cos(2.0 * math.pi / COEFFS * (frequency[:, None] * positions[None, :]) + phases[:, None])
        noise_part = jax.random.normal(key_factor, (factor_count, COEFFS), jnp.float32)
        columns = factor_scale * (noise_part + wave_part)

        def add_term(step, running):
            column = lax.dynamic_index_in_dim(columns, step, 0, keepdims=False)
            return running + column[:, None] * column[None, :]
        matrix = lax.fori_loop(0, factor_count, add_term, matrix)
        return matrix.astype(jnp.bfloat16)
    return lax.map(month, jnp.arange(MONTHS, dtype=jnp.int32))


def levels(rng, shape, cuts, least, high):
    factor_of = 1.0
    for dim, blocks in cuts:
        heights = jax.random.uniform(jax.random.fold_in(jax.random.fold_in(rng, 6), dim), (blocks,), jnp.float32, least / len(cuts), high / len(cuts))
        factor_of = factor_of * jnp.repeat(jnp.exp(heights), shape[dim] // blocks).reshape((-1,) + (1,) * (len(shape) - 1 - dim))
    return factor_of


def noise(rng, shape, deviation, reach, pieces=(), kind=jnp.bfloat16):
    array = deviation * jax.random.normal(rng, shape, jnp.float32)
    if pieces:
        array = array * levels(rng, shape, pieces, -0.22, 0.18)
    return jnp.clip(array, -reach, reach).astype(kind)


def setup_inputs(seed: int = 0) -> dict:
    splits = jax.random.split(jax.random.key(seed), 6)
    return {
        "solution": noise(splits[0], (MONTHS, RHS, COEFFS), 1.0, 6.0, ((0, 4), (2, 8)), jnp.float32),
        "residual": noise(splits[1], (MONTHS, RHS, COEFFS), 1.0, 6.0, ((0, 4), (2, 8)), jnp.float32),
        "direction": noise(splits[2], (MONTHS, RHS, COEFFS), 1.0, 6.0, ((0, 4), (2, 8)), jnp.float32),
        "normal": draw_normal(jax.random.fold_in(splits[5], 71), 0),
        "weights": jnp.clip(jnp.exp(math.log(3.0) - 2.3025851 * jax.random.uniform(splits[4], (COEFFS,), jnp.float32) ** levels(splits[4], (COEFFS,), ((0, 8),), -0.2, 0.2)), 0.3, 3.0),
    }


HIGH = lax.Precision.HIGHEST

def solve_spd(matrix, rhs):
    lower = jnp.linalg.cholesky(matrix)
    inner = lax.linalg.triangular_solve(lower, rhs, left_side=True, lower=True, transpose_a=False)
    return lax.linalg.triangular_solve(lower, inner, left_side=True, lower=True, transpose_a=True)

def gram_of(left, right):
    return jnp.einsum('trp,tsp->rs', left, right, precision=HIGH)

def combine(coeffs, blocks):
    return jnp.einsum('rs,trp->tsp', coeffs, blocks, precision=HIGH)

def reference(solution, residual, direction, normal, weights):
    dir_low = direction.astype(jnp.bfloat16)

    def month_product(pair):
        block, vectors = pair
        return lax.dot_general(vectors.astype(jnp.float32), block.astype(jnp.float32), (((1,), (1,)), ((), ())), preferred_element_type=jnp.float32)
    product = lax.map(month_product, (normal, dir_low))
    centre = dir_low.astype(jnp.float32)
    zero = jnp.zeros_like(centre[:1])
    prev = jnp.concatenate([zero, centre[:-1]], axis=0)
    after = jnp.concatenate([centre[1:], zero], axis=0)
    month_idx = jnp.arange(MONTHS, dtype=jnp.int32)
    has_prev = (month_idx > 0).astype(jnp.float32)[:, None, None]
    has_next = (month_idx < MONTHS - 1).astype(jnp.float32)[:, None, None]
    coupled = has_prev * (centre - prev) + has_next * (centre - after)
    image = product + weights[None, None, :] * coupled
    gram_old = gram_of(residual, residual)
    gram_old = 0.5 * (gram_old + gram_old.T)
    curvature = gram_of(direction, image)
    curvature = 0.5 * (curvature + curvature.T)
    alpha = solve_spd(curvature, gram_old)
    new_solution = solution + combine(alpha, direction)
    new_residual = residual - combine(alpha, image)
    gram_new = gram_of(new_residual, new_residual)
    beta = solve_spd(gram_old, gram_new)
    new_direction = new_residual + combine(beta, direction)
    return (new_solution, new_residual, new_direction)
```

```python
import functools

import jax
import jax.numpy as jnp
from jax import lax
from jax.experimental import pallas as pl
from jax.experimental.pallas import tpu as pltpu
from jax.sharding import PartitionSpec as P

HIGH = lax.Precision.HIGHEST
ROWS_BY_ROWS = (((1,), (1,)), ((), ()))
SMEM = pl.BlockSpec(memory_space=pltpu.SMEM)
VMEM = pl.BlockSpec(memory_space=pltpu.VMEM)
HBM = pl.BlockSpec(memory_space=pltpu.HBM)
TILE = 256


def dot_nt(left, right):
    return lax.dot_general(left, right, ROWS_BY_ROWS, precision=HIGH, preferred_element_type=jnp.float32)


def dot_nn(left, right):
    return jnp.dot(left, right, precision=HIGH, preferred_element_type=jnp.float32)


def round_kernel(wide_ref, low_ref):
    low_ref[...] = wide_ref[...].astype(jnp.bfloat16)


def place_kernel(slots_ref, _, *refs):
    *parts, out_ref = refs
    width = parts[0].shape[1]
    for i, part in enumerate(parts):
        out_ref[:, pl.ds(pl.multiple_of(slots_ref[i] * width, width), width)] = part[...]


def product_of(places_ref, blocks, slab_ref, sum_ref, out_ref):
    rows = slab_ref.shape[0]
    width = blocks[0].shape[1]
    tile = min(TILE, rows)
    for start in range(0, rows, tile):
        part = pl.ds(start, tile)
        total = None if sum_ref is None else sum_ref[:, part]
        for i, block in enumerate(blocks):
            columns = pl.ds(pl.multiple_of(places_ref[i] * width, width), width)
            term = lax.dot_general(
                block[...], slab_ref[part, columns], ROWS_BY_ROWS, preferred_element_type=jnp.float32
            )
            total = term if total is None else total + term
        out_ref[:, part] = total


def first_kernel(places_ref, block_ref, next_ref, low_ref, slab_ref, out_ref, low_out_ref):
    low_out_ref[...] = low_ref[...]
    product_of(places_ref, [block_ref, next_ref], slab_ref, None, out_ref)


def image_kernel(count, places_ref, ends_ref, *refs):
    blocks, refs = refs[:count], refs[count:]
    slab_ref, sum_ref, dirs_ref, resid_ref, before_ref, after_ref, weights_ref = refs[:7]
    image_ref, grams_ref = refs[7:]
    dirs = dirs_ref[...]
    resid = resid_ref[...]
    centre = dirs.astype(jnp.bfloat16).astype(jnp.float32)
    has_prev = ends_ref[0].astype(jnp.float32)
    has_next = ends_ref[1].astype(jnp.float32)
    coupled = has_prev * (centre - before_ref[...].astype(jnp.float32)) + has_next * (
        centre - after_ref[...].astype(jnp.float32)
    )
    image_ref[...] = sum_ref[...] + weights_ref[...] * coupled
    product_of(places_ref, blocks, slab_ref, image_ref, image_ref)
    image = image_ref[...]
    left = jnp.concatenate([resid, dirs, image], axis=0)
    right = jnp.concatenate([resid, image], axis=0)
    grams = dot_nt(left, right)
    rhs = resid.shape[0]
    grams_ref[...] = jnp.concatenate([grams[:rhs], grams[rhs : 2 * rhs], grams[2 * rhs :]], axis=1)


def right_divide(*systems):
    size = systems[0][0].shape[0]
    works = [jnp.concatenate(system, axis=0) for system in systems]
    lane = lax.broadcasted_iota(jnp.int32, works[0].shape, 1)
    for k in range(size):
        for i, work in enumerate(works):
            row = work[k : k + 1, :]
            column = work[:, k : k + 1]
            inverse = 1.0 / work[k : k + 1, k : k + 1]
            scaled = jnp.where(lane[:1] == k, -inverse, row * inverse)
            works[i] = jnp.where(lane == k, 0.0, work) - column * scaled
    return [work[size:] for work in works]


def update_kernel(*refs):
    *gram_refs, solution_ref, resid_ref, dirs_ref, image_ref, next_solution_ref, next_resid_ref, next_dirs_ref = refs
    grams = sum((ref[...] for ref in gram_refs[1:]), gram_refs[0][...])
    rhs = grams.shape[0]
    rr, rq, _, dq, qr, qq = (grams[:, i * rhs : (i + 1) * rhs] for i in range(6))
    old = 0.5 * (rr + rr.T)
    curvature = 0.5 * (dq + dq.T)
    rows = lax.broadcasted_iota(jnp.int32, (rhs, rhs), 0)
    cols = lax.broadcasted_iota(jnp.int32, (rhs, rhs), 1)
    unit = jnp.where(rows == cols, 1.0, 0.0).astype(jnp.float32)
    alpha_t, old_inverse = right_divide((curvature, old), (old, unit))
    new = rr - dot_nn(alpha_t, qr) + dot_nt(dot_nn(alpha_t, qq) - rq, alpha_t)
    beta_t = dot_nn(new, old_inverse)
    dirs = dirs_ref[...]
    next_resid = resid_ref[...] - dot_nn(alpha_t, image_ref[...])
    next_resid_ref[...] = next_resid
    next_solution_ref[...] = solution_ref[...] + dot_nn(alpha_t, dirs)
    next_dirs_ref[...] = next_resid + dot_nn(beta_t, dirs)


def exchanged(value, axis, stride):
    return lax.ppermute(value, axis, [(i, i ^ stride) for i in range(lax.axis_size(axis))])


def rounds(count):
    bits = [1 << i for i in range((count - 1).bit_length())]
    groups = [bits[:1]] + [bits[i : i + 2] for i in range(1, len(bits), 2)] if len(bits) % 2 else [bits[i : i + 2] for i in range(0, len(bits), 2)]
    return [[group[0]] if len(group) == 1 else [group[0], group[1], group[0] + group[1]] for group in groups]


def gathered(block, index, strides, slab):
    parts = [block] + [exchanged(block, "row", stride) for stride in strides]
    count = len(parts)
    shift = strides[0].bit_length() - 1
    slots = jnp.stack([((index ^ stride) >> shift) & (count - 1) for stride in (0, *strides)])
    return pl.pallas_call(
        place_kernel,
        in_specs=[SMEM, HBM] + [VMEM] * count,
        out_specs=VMEM,
        out_shape=jax.ShapeDtypeStruct((block.shape[0], count * block.shape[1]), block.dtype),
        compiler_params=pltpu.CompilerParams(vmem_limit_bytes=2 << 20),
        name="place",
    )(slots, slab, *parts)


def local(solution, residual, direction, normal, weights):
    rhs, count = direction.shape[1:]
    dirs, resid = direction[0], residual[0]
    slab = pltpu.with_memory_space_constraint(normal[0], pltpu.HBM)
    low_type = jax.ShapeDtypeStruct((rhs, count), jnp.bfloat16)
    own_low = pl.pallas_call(
        round_kernel,
        in_specs=[VMEM],
        out_specs=VMEM,
        out_shape=low_type,
        compiler_params=pltpu.CompilerParams(vmem_limit_bytes=2 << 20),
        name="low",
    )(dirs)
    row = lax.axis_index("row")
    *near, far = rounds(lax.axis_size("row"))
    block = own_low
    for strides in near:
        block = gathered(block, row, strides, slab)
    width = block.shape[1]
    blocks = [exchanged(block, "row", stride) for stride in far]
    shift = far[0].bit_length() - 1
    places = [row >> shift] + [(row ^ stride) >> shift for stride in far]
    months = lax.axis_size("tm")
    month = lax.axis_index("tm")

    wide = jax.ShapeDtypeStruct((rhs, count), jnp.float32)
    params = pltpu.CompilerParams(vmem_limit_bytes=8 << 20)
    product, own_low = pl.pallas_call(
        first_kernel,
        in_specs=[SMEM] + [VMEM] * 4,
        out_specs=[VMEM] * 2,
        out_shape=[wide, low_type],
        compiler_params=params,
        cost_estimate=pl.CostEstimate(flops=2 * rhs * count * width, bytes_accessed=2 * count * width, transcendentals=0),
        name="first",
    )(jnp.stack(places[:2]), block, blocks[0], own_low, normal[0])
    before = lax.ppermute(own_low, "tm", [(i, i + 1) for i in range(months - 1)])
    after = lax.ppermute(own_low, "tm", [(i + 1, i) for i in range(months - 1)])
    late = blocks[1:]
    image, grams = pl.pallas_call(
        functools.partial(image_kernel, len(late)),
        in_specs=[SMEM] * 2 + [VMEM] * (len(late) + 7),
        out_specs=[VMEM] * 2,
        out_shape=[wide, jax.ShapeDtypeStruct((rhs, 6 * rhs), jnp.float32)],
        compiler_params=params,
        name="image",
    )(
        jnp.stack(places[2:]), jnp.stack([month > 0, month < months - 1]).astype(jnp.int32),
        *late, normal[0], product, dirs, resid, before, after, weights[None],
    )
    steps = [(axis, strides) for axis in ("row", "tm") for strides in rounds(lax.axis_size(axis))]
    parts = [grams]
    for axis, strides in steps:
        total = functools.reduce(jnp.add, parts)
        parts = [total] + [exchanged(total, axis, stride) for stride in strides]
    outs = pl.pallas_call(
        update_kernel,
        in_specs=[VMEM] * (len(parts) + 4),
        out_specs=[VMEM] * 3,
        out_shape=[wide] * 3,
        compiler_params=params,
        name="update",
    )(*parts, solution[0], resid, dirs, image)
    return tuple(out[None] for out in outs)


def solution(mesh):
    placed = (
        P("tm", None, "row"),
        P("tm", None, "row"),
        P("tm", None, "row"),
        P("tm", "row", None),
        P("row"),
    )
    return jax.shard_map(
        local,
        mesh=mesh,
        in_specs=placed,
        out_specs=(P("tm", None, "row"), P("tm", None, "row"), P("tm", None, "row")),
        check_vma=False,
    )
```

```python
import functools

import jax
import jax.numpy as jnp
from jax import lax
from jax.experimental import pallas as pl
from jax.experimental.pallas import tpu as pltpu
from jax.sharding import PartitionSpec as P

HIGH = lax.Precision.HIGHEST
ROWS_BY_ROWS = (((1,), (1,)), ((), ()))
SMEM = pl.BlockSpec(memory_space=pltpu.SMEM)
VMEM = pl.BlockSpec(memory_space=pltpu.VMEM)
HBM = pl.BlockSpec(memory_space=pltpu.HBM)
TILE = 256


def dot_nt(left, right):
    return lax.dot_general(left, right, ROWS_BY_ROWS, precision=HIGH, preferred_element_type=jnp.float32)


def dot_nn(left, right):
    return jnp.dot(left, right, precision=HIGH, preferred_element_type=jnp.float32)


def rounded(ref):
    return ref[...].astype(jnp.bfloat16).astype(jnp.float32)


def place_kernel(count, *refs):
    slots, parts, out_ref = refs[:count], refs[count + 1 : 2 * count + 1], refs[-1]
    width = parts[0].shape[1]
    for slot, part in zip(slots, parts, strict=True):
        out_ref[:, pl.ds(pl.multiple_of(slot[0] * width, width), width)] = part[...].astype(out_ref.dtype)


def product_of(places, blocks, slab_ref, sum_ref, out_ref):
    rows = slab_ref.shape[0]
    width = blocks[0].shape[1]
    tile = min(TILE, rows)
    for start in range(0, rows, tile):
        part = pl.ds(start, tile)
        total = None if sum_ref is None else sum_ref[:, part]
        for i, block in enumerate(blocks):
            columns = pl.ds(pl.multiple_of(places[i][0] * width, width), width)
            term = lax.dot_general(
                block[...], slab_ref[part, columns], ROWS_BY_ROWS, preferred_element_type=jnp.float32
            )
            total = term if total is None else total + term
        out_ref[:, part] = total


def first_kernel(place_ref, next_place_ref, block_ref, next_ref, slab_ref, _, out_ref):
    product_of([place_ref, next_place_ref], [block_ref, next_ref], slab_ref, None, out_ref)


def image_kernel(count, *refs):
    places, blocks, refs = refs[:count], refs[count : 2 * count], refs[2 * count :]
    has_before_ref, has_after_ref, slab_ref, sum_ref, dirs_ref, resid_ref, before_ref, after_ref, weights_ref = refs[:9]
    image_ref, grams_ref = refs[9:]
    dirs = dirs_ref[...]
    resid = resid_ref[...]
    centre = rounded(dirs_ref)
    has_before = has_before_ref[0].astype(jnp.float32)
    has_after = has_after_ref[0].astype(jnp.float32)
    coupled = has_before * (centre - rounded(before_ref)) + has_after * (centre - rounded(after_ref))
    image_ref[...] = sum_ref[...] + weights_ref[...] * coupled
    product_of(places, blocks, slab_ref, image_ref, image_ref)
    image = image_ref[...]
    left = jnp.concatenate([resid, dirs, image], axis=0)
    right = jnp.concatenate([resid, image], axis=0)
    grams = dot_nt(left, right)
    rhs = resid.shape[0]
    grams_ref[...] = jnp.concatenate([grams[:rhs], grams[rhs : 2 * rhs], grams[2 * rhs :]], axis=1)


def right_divide(*systems):
    size = systems[0][0].shape[0]
    works = [jnp.concatenate(system, axis=0) for system in systems]
    lane = lax.broadcasted_iota(jnp.int32, works[0].shape, 1)
    for k in range(size):
        for i, work in enumerate(works):
            row = work[k : k + 1, :]
            column = work[:, k : k + 1]
            inverse = 1.0 / work[k : k + 1, k : k + 1]
            scaled = jnp.where(lane[:1] == k, -inverse, row * inverse)
            works[i] = jnp.where(lane == k, 0.0, work) - column * scaled
    return [work[size:] for work in works]


def update_kernel(*refs):
    *gram_refs, solution_ref, resid_ref, dirs_ref, image_ref, next_solution_ref, next_resid_ref, next_dirs_ref = refs
    grams = sum((ref[...] for ref in gram_refs[1:]), gram_refs[0][...])
    rhs = grams.shape[0]
    rr, rq, _, dq, qr, qq = (grams[:, i * rhs : (i + 1) * rhs] for i in range(6))
    old = 0.5 * (rr + rr.T)
    curvature = 0.5 * (dq + dq.T)
    rows = lax.broadcasted_iota(jnp.int32, (rhs, rhs), 0)
    cols = lax.broadcasted_iota(jnp.int32, (rhs, rhs), 1)
    unit = jnp.where(rows == cols, 1.0, 0.0).astype(jnp.float32)
    alpha_t, old_inverse = right_divide((curvature, old), (old, unit))
    new = rr - dot_nn(alpha_t, qr) + dot_nt(dot_nn(alpha_t, qq) - rq, alpha_t)
    beta_t = dot_nn(new, old_inverse)
    dirs = dirs_ref[...]
    next_resid = resid_ref[...] - dot_nn(alpha_t, image_ref[...])
    next_resid_ref[...] = next_resid
    next_solution_ref[...] = solution_ref[...] + dot_nn(alpha_t, dirs)
    next_dirs_ref[...] = next_resid + dot_nn(beta_t, dirs)


def exchanged(value, axis, stride):
    return lax.ppermute(value, axis, [(i, i ^ stride) for i in range(lax.axis_size(axis))])


def rounds(count):
    bits = [1 << i for i in range((count - 1).bit_length())]
    groups = [bits[:1]] + [bits[i : i + 2] for i in range(1, len(bits), 2)] if len(bits) % 2 else [bits[i : i + 2] for i in range(0, len(bits), 2)]
    return [[group[0]] if len(group) == 1 else [group[0], group[1], group[0] + group[1]] for group in groups]


def scalar(value):
    return jnp.asarray(value, jnp.int32).reshape(1)


def gathered(block, index, strides, slab):
    parts = [block] + [exchanged(block, "row", stride) for stride in strides]
    count = len(parts)
    shift = strides[0].bit_length() - 1
    slots = [scalar(((index ^ stride) >> shift) & (count - 1)) for stride in (0, *strides)]
    return pl.pallas_call(
        functools.partial(place_kernel, count),
        in_specs=[SMEM] * count + [HBM] + [VMEM] * count,
        out_specs=VMEM,
        out_shape=jax.ShapeDtypeStruct((block.shape[0], count * block.shape[1]), jnp.bfloat16),
        compiler_params=pltpu.CompilerParams(vmem_limit_bytes=2 << 20),
        name="place",
    )(*slots, slab, *parts)


def local(solution, residual, direction, normal, weights):
    rhs, count = direction.shape[1:]
    dirs, resid = direction[0], residual[0]
    slab = pltpu.with_memory_space_constraint(normal[0], pltpu.HBM)
    row = lax.axis_index("row")
    *near, far = rounds(lax.axis_size("row"))
    block = dirs
    for strides in near:
        block = gathered(block, row, strides, slab)
    width = block.shape[1]
    blocks = [exchanged(block, "row", stride) for stride in far]
    shift = far[0].bit_length() - 1
    places = [scalar((row ^ stride) >> shift) for stride in (0, *far)]
    months = lax.axis_size("tm")
    month = lax.axis_index("tm")

    wide = jax.ShapeDtypeStruct((rhs, count), jnp.float32)
    params = pltpu.CompilerParams(vmem_limit_bytes=8 << 20)
    product = pl.pallas_call(
        first_kernel,
        in_specs=[SMEM] * 2 + [VMEM] * 4,
        out_specs=VMEM,
        out_shape=wide,
        compiler_params=params,
        cost_estimate=pl.CostEstimate(flops=2 * rhs * count * width, bytes_accessed=2 * count * width, transcendentals=0),
        name="first",
    )(*places[:2], block, blocks[0], normal[0], jnp.concatenate(places))
    pairs = [[(i, i + 1) for i in range(first, months - 1, 2)] for first in (0, 1)]
    before, after = (lax.ppermute(dirs, "tm", [way for i, j in pair for way in ((i, j), (j, i))]) for pair in pairs)
    late = blocks[1:]
    has_before = (month ^ 1) < months
    has_after = (month > 0) & ((month & 1 == 0) | (month < months - 1))
    image, grams = pl.pallas_call(
        functools.partial(image_kernel, len(late)),
        in_specs=[SMEM] * len(late) + [VMEM] * len(late) + [SMEM] * 2 + [VMEM] * 7,
        out_specs=[VMEM] * 2,
        out_shape=[wide, jax.ShapeDtypeStruct((rhs, 6 * rhs), jnp.float32)],
        compiler_params=params,
        name="image",
    )(
        *places[2:], *late, scalar(has_before), scalar(has_after),
        normal[0], product, dirs, resid, before, after, weights[None],
    )
    steps = [(axis, strides) for axis in ("row", "tm") for strides in rounds(lax.axis_size(axis))]
    parts = [grams]
    for axis, strides in steps:
        total = functools.reduce(jnp.add, parts)
        parts = [total] + [exchanged(total, axis, stride) for stride in strides]
    outs = pl.pallas_call(
        update_kernel,
        in_specs=[VMEM] * (len(parts) + 4),
        out_specs=[VMEM] * 3,
        out_shape=[wide] * 3,
        compiler_params=params,
        name="update",
    )(*parts, solution[0], resid, dirs, image)
    return tuple(out[None] for out in outs)


def solution(mesh):
    placed = (
        P("tm", None, "row"),
        P("tm", None, "row"),
        P("tm", None, "row"),
        P("tm", "row", None),
        P("row"),
    )
    return jax.shard_map(
        local,
        mesh=mesh,
        in_specs=placed,
        out_specs=(P("tm", None, "row"), P("tm", None, "row"), P("tm", None, "row")),
        check_vma=False,
    )
```

```python
import functools

import jax
import jax.numpy as jnp
from jax import lax
from jax.experimental import pallas as pl
from jax.experimental.pallas import tpu as pltpu
from jax.sharding import PartitionSpec as P

HIGH = lax.Precision.HIGHEST
ROWS_BY_ROWS = (((1,), (1,)), ((), ()))
SMEM = pl.BlockSpec(memory_space=pltpu.SMEM)
VMEM = pl.BlockSpec(memory_space=pltpu.VMEM)
HBM = pl.BlockSpec(memory_space=pltpu.HBM)
TILE = 256
SCALE_ROWS = 8
SMALLEST = 2.0**-126


def dot_nt(left, right):
    return lax.dot_general(left, right, ROWS_BY_ROWS, precision=HIGH, preferred_element_type=jnp.float32)


def dot_nn(left, right):
    return jnp.dot(left, right, precision=HIGH, preferred_element_type=jnp.float32)


def mark_kernel(_, out_ref):
    out_ref[...] = jnp.zeros(out_ref.shape, out_ref.dtype)


def rounded(ref):
    return ref[...].astype(jnp.bfloat16).astype(jnp.float32)


def place_kernel(count, *refs):
    slots, parts, out_ref = refs[:count], refs[count + 1 : 2 * count + 1], refs[-1]
    width = parts[0].shape[1]
    for slot, part in zip(slots, parts, strict=True):
        out_ref[:, pl.ds(pl.multiple_of(slot[0] * width, width), width)] = part[...].astype(out_ref.dtype)


def product_of(places, blocks, slab_ref, sum_ref, out_ref):
    rows = slab_ref.shape[0]
    width = blocks[0].shape[1]
    tile = min(TILE, rows)
    for start in range(0, rows, tile):
        part = pl.ds(start, tile)
        total = None if sum_ref is None else sum_ref[:, part]
        for i, block in enumerate(blocks):
            columns = pl.ds(pl.multiple_of(places[i][0] * width, width), width)
            term = lax.dot_general(
                block[...], slab_ref[part, columns], ROWS_BY_ROWS, preferred_element_type=jnp.float32
            )
            total = term if total is None else total + term
        out_ref[:, part] = total


def first_kernel(place_ref, next_place_ref, block_ref, next_ref, slab_ref, _, out_ref):
    product_of([place_ref, next_place_ref], [block_ref, next_ref], slab_ref, None, out_ref)


def image_kernel(count, *refs):
    places, blocks, refs = refs[:count], refs[count : 2 * count], refs[2 * count :]
    has_before_ref, has_after_ref, slab_ref, sum_ref, dirs_ref, resid_ref, before_ref, after_ref, weights_ref = refs[:9]
    image_ref, grams_ref = refs[9:]
    dirs = dirs_ref[...]
    resid = resid_ref[...]
    centre = rounded(dirs_ref)
    has_before = has_before_ref[0].astype(jnp.float32)
    has_after = has_after_ref[0].astype(jnp.float32)
    coupled = has_before * (centre - rounded(before_ref)) + has_after * (centre - rounded(after_ref))
    image_ref[...] = sum_ref[...] + weights_ref[...] * coupled
    product_of(places, blocks, slab_ref, image_ref, image_ref)
    image = image_ref[...]
    rhs = resid.shape[0]
    straight = dot_nt(jnp.concatenate([resid, dirs], axis=0), jnp.concatenate([resid, image], axis=0))
    scale = jnp.maximum(jnp.max(jnp.abs(image), keepdims=True), SMALLEST)
    scaled = image * (1.0 / scale)
    across = dot_nt(scaled, jnp.concatenate([resid, scaled], axis=0))
    grams_ref[:rhs, :] = jnp.concatenate([straight[:rhs], straight[rhs:], across], axis=1)
    grams_ref[rhs:, :] = jnp.broadcast_to(scale, (SCALE_ROWS, 6 * rhs))


def total(refs):
    rhs = refs[0].shape[0] - SCALE_ROWS
    scales = [ref[rhs : rhs + 1, :] for ref in refs]
    scale = functools.reduce(jnp.maximum, scales)
    block = lax.broadcasted_iota(jnp.int32, scale.shape, 1) // rhs
    out = 0.0
    for ref, own in zip(refs, scales, strict=True):
        ratio = own / scale
        factor = jnp.where(block == 5, ratio * ratio, jnp.where(block == 4, ratio, 1.0))
        out = out + ref[:rhs, :] * factor
    return out, scale


def total_kernel(*refs):
    *parts, out_ref = refs
    grams, scale = total(parts)
    out_ref[: grams.shape[0], :] = grams
    out_ref[grams.shape[0] :, :] = jnp.broadcast_to(scale, (SCALE_ROWS, grams.shape[1]))


def reciprocal(value):
    guess = pl.reciprocal(value, approx=True)
    for _ in range(2):
        guess = guess * (2.0 - value * guess)
    return guess


def right_divide(*systems):
    size = systems[0][0].shape[0]
    works = [jnp.concatenate(system, axis=0) for system in systems]
    lane = lax.broadcasted_iota(jnp.int32, works[0].shape, 1)
    for k in range(0, size, 2):
        here, after = lane == k, lane == k + 1
        for i, work in enumerate(works):
            first = jnp.broadcast_to(work[:, k : k + 1], work.shape)
            second = jnp.broadcast_to(work[:, k + 1 : k + 2], work.shape)
            over = first[k : k + 1]
            under = first[k + 1 : k + 2]
            beside = second[k : k + 1]
            inverse = reciprocal(over)
            ratio = under * inverse
            inverse_next = reciprocal(second[k + 1 : k + 2] - ratio * beside)
            top = jnp.where(here[:1], -1.0, jnp.where(after[:1], 0.0, work[k : k + 1]))
            low = jnp.where(here[:1], 0.0, jnp.where(after[:1], -1.0, work[k + 1 : k + 2]))
            low = (low - ratio * top) * inverse_next
            top = (top - beside * low) * inverse
            works[i] = jnp.where(here | after, 0.0, work) - first * top - second * low
    return [work[size:] for work in works]


def update_kernel(*refs):
    *gram_refs, solution_ref, resid_ref, dirs_ref, image_ref, next_solution_ref, next_resid_ref, next_dirs_ref = refs
    grams, scale = total(gram_refs)
    rhs = grams.shape[0]
    rr, _, _, dq, qr, qq = (grams[:, i * rhs : (i + 1) * rhs] for i in range(6))
    old = 0.5 * (rr + rr.T)
    curvature = 0.5 * (dq + dq.T)
    rows = lax.broadcasted_iota(jnp.int32, (rhs, rhs), 0)
    cols = lax.broadcasted_iota(jnp.int32, (rhs, rhs), 1)
    unit = jnp.where(rows == cols, 1.0, 0.0).astype(jnp.float32)
    alpha_t, old_inverse = right_divide((curvature, old), (old, unit))
    scaled_t = alpha_t * scale[:, :rhs]
    dirs = dirs_ref[...]
    apart = dot_nn(old_inverse, dirs)
    new = rr - dot_nn(scaled_t, qr) + dot_nt(dot_nn(scaled_t, qq) - qr.T, scaled_t)
    next_resid = resid_ref[...] - dot_nn(alpha_t, image_ref[...])
    next_resid_ref[...] = next_resid
    next_solution_ref[...] = solution_ref[...] + dot_nn(alpha_t, dirs)
    next_dirs_ref[...] = next_resid + dot_nn(new, apart)


def exchanged(value, axis, stride):
    return lax.ppermute(value, axis, [(i, i ^ stride) for i in range(lax.axis_size(axis))])


def rounds(count):
    bits = [1 << i for i in range((count - 1).bit_length())]
    groups = [bits[:1]] + [bits[i : i + 2] for i in range(1, len(bits), 2)] if len(bits) % 2 else [bits[i : i + 2] for i in range(0, len(bits), 2)]
    return [[group[0]] if len(group) == 1 else [group[0], group[1], group[0] + group[1]] for group in groups]


def scalar(value):
    return jnp.asarray(value, jnp.int32).reshape(1)


def gathered(block, index, strides, slab):
    parts = [block] + [exchanged(block, "row", stride) for stride in strides]
    count = len(parts)
    shift = strides[0].bit_length() - 1
    slots = [scalar(((index ^ stride) >> shift) & (count - 1)) for stride in (0, *strides)]
    return pl.pallas_call(
        functools.partial(place_kernel, count),
        in_specs=[SMEM] * count + [VMEM] * (count + 1),
        out_specs=VMEM,
        out_shape=jax.ShapeDtypeStruct((block.shape[0], count * block.shape[1]), jnp.bfloat16),
        compiler_params=pltpu.CompilerParams(vmem_limit_bytes=2 << 20),
        name="place",
    )(*slots, slab, *parts)


def local(solution, residual, direction, normal, weights):
    rhs, count = direction.shape[1:]
    dirs, resid = direction[0], residual[0]
    slab = pltpu.with_memory_space_constraint(normal[0], pltpu.HBM)
    mark = pl.pallas_call(
        mark_kernel,
        in_specs=[HBM],
        out_specs=VMEM,
        out_shape=jax.ShapeDtypeStruct((8, 128), jnp.float32),
        compiler_params=pltpu.CompilerParams(vmem_limit_bytes=2 << 20),
        name="mark",
    )(slab)
    row = lax.axis_index("row")
    *near, far = rounds(lax.axis_size("row"))
    block = dirs
    for strides in near:
        block = gathered(block, row, strides, mark)
    width = block.shape[1]
    blocks = [exchanged(block, "row", stride) for stride in far]
    shift = far[0].bit_length() - 1
    places = [scalar((row ^ stride) >> shift) for stride in (0, *far)]
    months = lax.axis_size("tm")
    month = lax.axis_index("tm")

    wide = jax.ShapeDtypeStruct((rhs, count), jnp.float32)
    gram_type = jax.ShapeDtypeStruct((rhs + SCALE_ROWS, 6 * rhs), jnp.float32)
    params = pltpu.CompilerParams(vmem_limit_bytes=8 << 20)
    product = pl.pallas_call(
        first_kernel,
        in_specs=[SMEM] * 2 + [VMEM] * 4,
        out_specs=VMEM,
        out_shape=wide,
        compiler_params=params,
        cost_estimate=pl.CostEstimate(flops=2 * rhs * count * width, bytes_accessed=2 * count * width, transcendentals=0),
        name="first",
    )(*places[:2], block, blocks[0], normal[0], jnp.concatenate(places))
    pairs = [[(i, i + 1) for i in range(first, months - 1, 2)] for first in (0, 1)]
    before, after = (lax.ppermute(dirs, "tm", [way for i, j in pair for way in ((i, j), (j, i))]) for pair in pairs)
    late = blocks[1:]
    has_before = (month ^ 1) < months
    has_after = (month > 0) & ((month & 1 == 0) | (month < months - 1))
    image, grams = pl.pallas_call(
        functools.partial(image_kernel, len(late)),
        in_specs=[SMEM] * len(late) + [VMEM] * len(late) + [SMEM] * 2 + [VMEM] * 7,
        out_specs=[VMEM] * 2,
        out_shape=[wide, gram_type],
        compiler_params=params,
        name="image",
    )(
        *places[2:], *late, scalar(has_before), scalar(has_after),
        normal[0], product, dirs, resid, before, after, weights[None],
    )
    steps = [(axis, strides) for axis in ("row", "tm") for strides in rounds(lax.axis_size(axis))]
    parts = [grams]
    for axis, strides in steps:
        if len(parts) > 1:
            grams = pl.pallas_call(
                total_kernel,
                in_specs=[VMEM] * len(parts),
                out_specs=VMEM,
                out_shape=gram_type,
                compiler_params=pltpu.CompilerParams(vmem_limit_bytes=2 << 20),
                name="total",
            )(*parts)
        parts = [grams] + [exchanged(grams, axis, stride) for stride in strides]
    outs = pl.pallas_call(
        update_kernel,
        in_specs=[VMEM] * (len(parts) + 4),
        out_specs=[VMEM] * 3,
        out_shape=[wide] * 3,
        compiler_params=params,
        name="update",
    )(*parts, solution[0], resid, dirs, image)
    return tuple(out[None] for out in outs)


def solution(mesh):
    placed = (
        P("tm", None, "row"),
        P("tm", None, "row"),
        P("tm", None, "row"),
        P("tm", "row", None),
        P("row"),
    )
    return jax.shard_map(
        local,
        mesh=mesh,
        in_specs=placed,
        out_specs=(P("tm", None, "row"), P("tm", None, "row"), P("tm", None, "row")),
        check_vma=False,
    )
```

```python
import functools

import jax
import jax.numpy as jnp
from jax import lax
from jax.experimental import pallas as pl
from jax.experimental.pallas import tpu as pltpu
from jax.sharding import PartitionSpec as P

HIGH = lax.Precision.HIGHEST
ROWS_BY_ROWS = (((1,), (1,)), ((), ()))
SMEM = pl.BlockSpec(memory_space=pltpu.SMEM)
VMEM = pl.BlockSpec(memory_space=pltpu.VMEM)
HBM = pl.BlockSpec(memory_space=pltpu.HBM)
TILE = 256
SCALE_ROWS = 8
SMALLEST = 2.0**-126


def dot_nt(left, right):
    return lax.dot_general(left, right, ROWS_BY_ROWS, precision=HIGH, preferred_element_type=jnp.float32)


def dot_nn(left, right):
    return jnp.dot(left, right, precision=HIGH, preferred_element_type=jnp.float32)


def mark_kernel(_, out_ref):
    out_ref[...] = jnp.zeros(out_ref.shape, out_ref.dtype)


def rounded(ref):
    return ref[...].astype(jnp.bfloat16).astype(jnp.float32)


def place_kernel(count, *refs):
    slots, parts, out_ref = refs[:count], refs[count + 1 : 2 * count + 1], refs[-1]
    width = parts[0].shape[1]
    for slot, part in zip(slots, parts, strict=True):
        out_ref[:, pl.ds(pl.multiple_of(slot[0] * width, width), width)] = part[...].astype(out_ref.dtype)


def product_of(places, blocks, slab_ref, sum_ref, out_ref):
    rows = slab_ref.shape[0]
    width = blocks[0].shape[1]
    tile = min(TILE, rows)
    for start in range(0, rows, tile):
        part = pl.ds(start, tile)
        total = None if sum_ref is None else sum_ref[:, part]
        for i, block in enumerate(blocks):
            columns = pl.ds(pl.multiple_of(places[i][0] * width, width), width)
            term = lax.dot_general(
                block[...], slab_ref[part, columns], ROWS_BY_ROWS, preferred_element_type=jnp.float32
            )
            total = term if total is None else total + term
        out_ref[:, part] = total


def first_kernel(place_ref, next_place_ref, block_ref, next_ref, slab_ref, _, out_ref):
    product_of([place_ref, next_place_ref], [block_ref, next_ref], slab_ref, None, out_ref)


def image_kernel(count, *refs):
    places, blocks, refs = refs[:count], refs[count : 2 * count], refs[2 * count :]
    has_before_ref, has_after_ref, slab_ref, sum_ref, dirs_ref, resid_ref, before_ref, after_ref, weights_ref = refs[:9]
    image_ref, grams_ref = refs[9:]
    dirs = dirs_ref[...]
    resid = resid_ref[...]
    centre = rounded(dirs_ref)
    has_before = has_before_ref[0].astype(jnp.float32)
    has_after = has_after_ref[0].astype(jnp.float32)
    coupled = has_before * (centre - rounded(before_ref)) + has_after * (centre - rounded(after_ref))
    image_ref[...] = sum_ref[...] + weights_ref[...] * coupled
    product_of(places, blocks, slab_ref, image_ref, image_ref)
    image = image_ref[...]
    rhs = resid.shape[0]
    straight = dot_nt(jnp.concatenate([resid, dirs], axis=0), jnp.concatenate([resid, image], axis=0))
    scale = jnp.maximum(jnp.max(jnp.abs(image), keepdims=True), SMALLEST)
    scaled = image * (1.0 / scale)
    across = dot_nt(scaled, jnp.concatenate([resid, scaled], axis=0))
    grams_ref[:rhs, :] = jnp.concatenate([straight[:rhs], straight[rhs:], across], axis=1)
    grams_ref[rhs:, :] = jnp.broadcast_to(scale, (SCALE_ROWS, 6 * rhs))


def total(refs):
    rhs = refs[0].shape[0] - SCALE_ROWS
    scales = [ref[rhs : rhs + 1, :] for ref in refs]
    scale = functools.reduce(jnp.maximum, scales)
    block = lax.broadcasted_iota(jnp.int32, scale.shape, 1) // rhs
    out = 0.0
    for ref, own in zip(refs, scales, strict=True):
        ratio = own / scale
        factor = jnp.where(block == 5, ratio * ratio, jnp.where(block == 4, ratio, 1.0))
        out = out + ref[:rhs, :] * factor
    return out, scale


def total_kernel(*refs):
    *parts, out_ref = refs
    grams, scale = total(parts)
    out_ref[: grams.shape[0], :] = grams
    out_ref[grams.shape[0] :, :] = jnp.broadcast_to(scale, (SCALE_ROWS, grams.shape[1]))


def reciprocal(value):
    guess = pl.reciprocal(value, approx=True)
    for _ in range(2):
        guess = guess * (2.0 - value * guess)
    return guess


def right_divide(*systems):
    size = systems[0][0].shape[0]
    works = [jnp.concatenate(system, axis=0) for system in systems]
    lane = lax.broadcasted_iota(jnp.int32, works[0].shape, 1)
    for k in range(0, size, 2):
        here, after = lane == k, lane == k + 1
        for i, work in enumerate(works):
            first = jnp.broadcast_to(work[:, k : k + 1], work.shape)
            second = jnp.broadcast_to(work[:, k + 1 : k + 2], work.shape)
            over = first[k : k + 1]
            under = first[k + 1 : k + 2]
            beside = second[k : k + 1]
            inverse = reciprocal(over)
            ratio = under * inverse
            inverse_next = reciprocal(second[k + 1 : k + 2] - ratio * beside)
            top = jnp.where(here[:1], -1.0, jnp.where(after[:1], 0.0, work[k : k + 1]))
            low = jnp.where(here[:1], 0.0, jnp.where(after[:1], -1.0, work[k + 1 : k + 2]))
            low = (low - ratio * top) * inverse_next
            top = (top - beside * low) * inverse
            works[i] = jnp.where(here | after, 0.0, work) - first * top - second * low
    return [work[size:] for work in works]


def update_kernel(*refs):
    *gram_refs, solution_ref, resid_ref, dirs_ref, image_ref, next_solution_ref, next_resid_ref, next_dirs_ref = refs
    grams, scale = total(gram_refs)
    rhs = grams.shape[0]
    rr, _, _, dq, qr, qq = (grams[:, i * rhs : (i + 1) * rhs] for i in range(6))
    old = 0.5 * (rr + rr.T)
    curvature = 0.5 * (dq + dq.T)
    rows = lax.broadcasted_iota(jnp.int32, (rhs, rhs), 0)
    cols = lax.broadcasted_iota(jnp.int32, (rhs, rhs), 1)
    unit = jnp.where(rows == cols, 1.0, 0.0).astype(jnp.float32)
    alpha_t, old_inverse = right_divide((curvature, old), (old, unit))
    scaled_t = alpha_t * scale[:, :rhs]
    dirs = dirs_ref[...]
    apart = dot_nn(old_inverse, dirs)
    new = rr - dot_nn(scaled_t, qr) + dot_nt(dot_nn(scaled_t, qq) - qr.T, scaled_t)
    next_resid = resid_ref[...] - dot_nn(alpha_t, image_ref[...])
    next_resid_ref[...] = next_resid
    next_solution_ref[...] = solution_ref[...] + dot_nn(alpha_t, dirs)
    next_dirs_ref[...] = next_resid + dot_nn(new, apart)


def exchanged(value, axis, stride):
    return lax.ppermute(value, axis, [(i, i ^ stride) for i in range(lax.axis_size(axis))])


def rounds(count, alone=0):
    bits = [1 << i for i in range((count - 1).bit_length())]
    first = [bits.pop(alone)] if len(bits) % 2 else []
    groups = [first] * len(first) + [bits[i : i + 2] for i in range(0, len(bits), 2)]
    return [group if len(group) == 1 else [*group, sum(group)] for group in groups]


def scalar(value):
    return jnp.asarray(value, jnp.int32).reshape(1)


def gathered(block, index, strides, slab):
    parts = [block] + [exchanged(block, "row", stride) for stride in strides]
    count = len(parts)
    shift = strides[0].bit_length() - 1
    slots = [scalar(((index ^ stride) >> shift) & (count - 1)) for stride in (0, *strides)]
    return pl.pallas_call(
        functools.partial(place_kernel, count),
        in_specs=[SMEM] * count + [VMEM] * (count + 1),
        out_specs=VMEM,
        out_shape=jax.ShapeDtypeStruct((block.shape[0], count * block.shape[1]), jnp.bfloat16),
        compiler_params=pltpu.CompilerParams(vmem_limit_bytes=2 << 20),
        name="place",
    )(*slots, slab, *parts)


def local(solution, residual, direction, normal, weights):
    rhs, count = direction.shape[1:]
    dirs, resid = direction[0], residual[0]
    slab = pltpu.with_memory_space_constraint(normal[0], pltpu.HBM)
    mark = pl.pallas_call(
        mark_kernel,
        in_specs=[HBM],
        out_specs=VMEM,
        out_shape=jax.ShapeDtypeStruct((8, 128), jnp.float32),
        compiler_params=pltpu.CompilerParams(vmem_limit_bytes=2 << 20),
        name="mark",
    )(slab)
    row = lax.axis_index("row")
    *near, far = rounds(lax.axis_size("row"))
    block = dirs
    for strides in near:
        block = gathered(block, row, strides, mark)
    width = block.shape[1]
    blocks = [exchanged(block, "row", stride) for stride in far]
    shift = far[0].bit_length() - 1
    places = [scalar((row ^ stride) >> shift) for stride in (0, *far)]
    months = lax.axis_size("tm")
    month = lax.axis_index("tm")

    wide = jax.ShapeDtypeStruct((rhs, count), jnp.float32)
    gram_type = jax.ShapeDtypeStruct((rhs + SCALE_ROWS, 6 * rhs), jnp.float32)
    params = pltpu.CompilerParams(vmem_limit_bytes=8 << 20)
    product = pl.pallas_call(
        first_kernel,
        in_specs=[SMEM] * 2 + [VMEM] * 4,
        out_specs=VMEM,
        out_shape=wide,
        compiler_params=params,
        cost_estimate=pl.CostEstimate(flops=2 * rhs * count * width, bytes_accessed=2 * count * width, transcendentals=0),
        name="first",
    )(*places[:2], block, blocks[0], normal[0], jnp.concatenate(places))
    pairs = [[(i, i + 1) for i in range(first, months - 1, 2)] for first in (0, 1)]
    before, after = (lax.ppermute(dirs, "tm", [way for i, j in pair for way in ((i, j), (j, i))]) for pair in pairs)
    late = blocks[1:]
    has_before = (month ^ 1) < months
    has_after = (month > 0) & ((month & 1 == 0) | (month < months - 1))
    image, grams = pl.pallas_call(
        functools.partial(image_kernel, len(late)),
        in_specs=[SMEM] * len(late) + [VMEM] * len(late) + [SMEM] * 2 + [VMEM] * 7,
        out_specs=[VMEM] * 2,
        out_shape=[wide, gram_type],
        compiler_params=params,
        name="image",
    )(
        *places[2:], *late, scalar(has_before), scalar(has_after),
        normal[0], product, dirs, resid, before, after, weights[None],
    )
    steps = [(axis, strides) for axis in ("row", "tm") for strides in rounds(lax.axis_size(axis), alone=-1)]
    parts = [grams]
    for axis, strides in steps:
        if len(parts) > 1:
            grams = pl.pallas_call(
                total_kernel,
                in_specs=[VMEM] * len(parts),
                out_specs=VMEM,
                out_shape=gram_type,
                compiler_params=pltpu.CompilerParams(vmem_limit_bytes=2 << 20),
                name="total",
            )(*parts)
        parts = [grams] + [exchanged(grams, axis, stride) for stride in strides]
    outs = pl.pallas_call(
        update_kernel,
        in_specs=[VMEM] * (len(parts) + 4),
        out_specs=[VMEM] * 3,
        out_shape=[wide] * 3,
        compiler_params=params,
        name="update",
    )(*parts, solution[0], resid, dirs, image)
    return tuple(out[None] for out in outs)


def solution(mesh):
    placed = (
        P("tm", None, "row"),
        P("tm", None, "row"),
        P("tm", None, "row"),
        P("tm", "row", None),
        P("row"),
    )
    return jax.shard_map(
        local,
        mesh=mesh,
        in_specs=placed,
        out_specs=(P("tm", None, "row"), P("tm", None, "row"), P("tm", None, "row")),
        check_vma=False,
    )
```
